512 devices in a mesh: dom: 512 (over x, z, y, core).
Axes of the slice: x: 4, y: 4, z: 16, core: 2. Of those that a mesh axis runs over, the one named last changes fastest.
Arguments:
- embeddings: float32 [524288, 256], P('dom'), may hold values from -1.5 to 1.5
- row_state: float32 [524288], P('dom'), may hold values from 0.005 to 0.05
- relations: float32 [256, 256], replicated, may hold values from -4 to 4
- rel_state: float32 [256], replicated, may hold values from 0.5 to 5
- plan: int32 [3], replicated, may hold values from 0 to 4
- edge_counts: int32 [3, 512], P(None, 'dom'), may hold values from 1 to 512, 131072 in all within a row
- sources: int32 [3, 262144], P(None, 'dom'), may hold values from 0 to 1023
- targets: int32 [3, 262144], P(None, 'dom'), may hold values from 0 to 1023
- relation_ids: int32 [3, 262144], P(None, 'dom'), may hold values from 0 to 255
- negatives: int32 [3, 512, 512], P(None, 'dom'), may hold values from 0 to 1023
Outputs:
- new_embeddings: float32 [524288, 256], P('dom')
- new_row_state: float32 [524288], P('dom')
- new_relations: float32 [256, 256], replicated
- new_rel_state: float32 [256], replicated
The draws below stay inside these ranges and needn't reach their ends.
Inputs may be any that keep to these rules, and one draw needn't show every extreme that they name: A partition's live edge slots in a round are its first edge_counts slots; the counts of one round sum to half of all slots.
All inputs are finite; a program needn't handle non-finite values. No bound on the sum of `edge_counts` on one device may be relied on, other than what follows from the above.
Results may differ from the reference program's by a relative error of at most 0.0003.
Values sent between devices are 32-bit elements; how exact they have to be, the bound alone decides.
A program may use at most 64 MiB of HBM per device.

```python
import math
import jax
import jax.numpy as jnp
import numpy as np
from jax import lax

W = 256
RELS = 256
ROWS = 1024
EDGES = 512
NEG = 512
ROUNDS = 3
BITS = 5
SPANS = 1
ENTITIES = 524288
N_DOM = 512


def plant(drawn, own_key, smallest, top_value):
    index_at = [jax.random.randint(jax.random.fold_in(own_key, axis), (), 0, length) for axis, length in enumerate(drawn.shape)]
    longest = drawn.shape.index(max(drawn.shape))
    neighbour = index_at[:longest] + [(index_at[longest] + 1) % drawn.shape[longest]] + index_at[longest + 1:]
    return drawn.at[tuple(index_at)].set(smallest).at[tuple(neighbour)].set(top_value)


def level_of(rng, shape, pieces, low, high):
    level, own = 1.0, jax.random.fold_in(rng, 6)
    for axis_at, parts in pieces:
        steps = jnp.exp(jax.random.uniform(jax.random.fold_in(own, axis_at), (parts,), jnp.float32, low / len(pieces), high / len(pieces)))
        level = level * jnp.repeat(steps, shape[axis_at] // parts).reshape([-1 if axis == axis_at else 1 for axis in range(len(shape))])
    return level


def split_up(count, total, most, skew):
    portions = [(1 << 20) // math.isqrt(rank ** skew) + 1 for rank in range(2, count + 1)]
    rest, holding = total - most - (count - 1), [1] * (count - 1)
    while rest > 0:
        free = [i for i in range(count - 1) if holding[i] < most]
        whole, remaining = sum([portions[i] for i in free]), rest
        for i in free:
            addition = min(most - holding[i], max(1, remaining * portions[i] // whole), rest)
            holding[i] = holding[i] + addition
            rest = rest - addition
    return np.array([most] + holding)


def uneven_parts(own_key, amount, total, bound, skew):
    if amount == 2:
        one = jax.random.randint(own_key, (), max(1, total - bound), min(bound, total - 1) + 1)
        return jnp.stack([one, total - one])
    sizes = jnp.asarray(split_up(amount, total, bound, skew), jnp.int32)
    pairs = (amount - 1) // 2
    source_of, receiver = sizes[1:1 + 2 * pairs:2], sizes[2:2 + 2 * pairs:2]
    slack = jnp.minimum(source_of - 1, bound - receiver)
    shifted = jax.random.randint(jax.random.fold_in(own_key, 1), (pairs,), 0, 1 << 20) % (slack + 1)
    sizes = sizes.at[1:1 + 2 * pairs:2].set(source_of - shifted).at[2:2 + 2 * pairs:2].set(receiver + shifted)
    return sizes[jax.random.permutation(jax.random.fold_in(own_key, 2), amount)]


def gaussian(stream_key, dims, scale, limit, shards=(), held_as=jnp.bfloat16):
    result = jax.random.normal(stream_key, dims, jnp.float32) * scale
    if len(shards) > 0:
        result = level_of(stream_key, dims, shards, -0.22, 0.18) * result
    return jnp.clip(result, min=-limit, max=limit).astype(held_as)


def setup_inputs(seed: int = 0) -> dict:
    keys = jax.random.split(jax.random.key(seed), 11)
    return {
        "embeddings": gaussian(keys[0], (ENTITIES, W), 0.25, 1.5, ((0, 512),), jnp.float32),
        "row_state": jnp.clip(jnp.exp(math.log(0.05) - 2.3025851 * jax.random.uniform(keys[1], (ENTITIES,), jnp.float32) ** level_of(keys[1], (ENTITIES,), ((0, 512),), -0.2, 0.2)), 0.005, 0.05),
        "relations": gaussian(keys[2], (RELS, W), 1.0, 4.0, (), jnp.float32),
        "rel_state": jnp.clip(jnp.exp(jax.random.uniform(keys[3], (RELS,), jnp.float32, math.log(0.5), math.log(5.0))), 0.5, 5.0),
        "plan": jax.random.randint(keys[4], (ROUNDS,), 0, BITS).astype(jnp.int32),
        "edge_counts": jax.vmap(lambda own: uneven_parts(own, N_DOM, EDGES * N_DOM // 2, EDGES, 2))(jax.random.split(keys[5], ROUNDS)).reshape((ROUNDS, N_DOM)).astype(jnp.int32),
        "sources": plant(jax.random.randint(keys[6], (ROUNDS, N_DOM * EDGES), 0, ROWS), jax.random.fold_in(keys[6], 1), 0, ROWS - 1).astype(jnp.int32),
        "targets": plant(jax.random.randint(keys[7], (ROUNDS, N_DOM * EDGES), 0, ROWS), jax.random.fold_in(keys[7], 1), 0, ROWS - 1).astype(jnp.int32),
        "relation_ids": plant(jax.random.randint(keys[8], (ROUNDS, N_DOM * EDGES), 0, RELS), jax.random.fold_in(keys[8], 1), 0, RELS - 1).astype(jnp.int32),
        "negatives": plant(jax.random.randint(keys[9], (ROUNDS, N_DOM * SPANS, NEG), 0, ROWS), jax.random.fold_in(keys[9], 1), 0, ROWS - 1).astype(jnp.int32),
    }


learn_rate = 0.1
highest = lax.Precision.HIGHEST

def bucket_grads(owned, partner, relations, source_ids, target_ids, kind_ids, negative_ids, count):
    live_mask = (jnp.arange(EDGES, dtype=jnp.int32) < count).astype(jnp.float32)
    rel_rows = relations[kind_ids]
    source = owned[source_ids]
    query = source * rel_rows * live_mask[:, None]
    target = partner[target_ids]
    flat_neg = negative_ids.reshape(-1)
    neg_rows = partner[flat_neg].reshape(SPANS, NEG, W)
    pos_score = lax.optimization_barrier(jnp.sum(query * target, axis=-1))
    pos_grad = -jax.nn.sigmoid(-pos_score)
    blocked = query.reshape(SPANS, NEG, W)
    scores = jnp.einsum('cew,ckw->cek', blocked, neg_rows, precision=highest)
    neg_grad = jax.nn.sigmoid(scores) / NEG
    spread = jnp.einsum('cek,ckw->cew', neg_grad, neg_rows, precision=highest).reshape(EDGES, W)
    query_grad = (pos_grad[:, None] * target + spread) * live_mask[:, None]
    target_grad = pos_grad[:, None] * query
    negrow_grad = jnp.einsum('cek,cew->ckw', neg_grad, blocked, precision=highest).reshape(EDGES, W)
    owned_grad = jnp.zeros((ROWS, W), jnp.float32).at[source_ids].add(query_grad * rel_rows)
    partner_grad = jnp.zeros((ROWS, W), jnp.float32).at[target_ids].add(target_grad).at[flat_neg].add(negrow_grad)
    rel_grad = jnp.zeros((RELS, W), jnp.float32).at[kind_ids].add(query_grad * source)
    return (owned_grad, partner_grad, rel_grad)

def adagrad(param, state, grad):
    state_new = state + lax.optimization_barrier(jnp.mean(grad * grad, axis=-1))
    return (param - learn_rate * grad / jnp.sqrt(state_new)[..., None], state_new)

def reference(embeddings, row_state, relations, rel_state, plan, edge_counts, sources, targets, relation_ids, negatives):
    blocks = embeddings.reshape(N_DOM, ROWS, W)
    states = row_state.reshape(N_DOM, ROWS)
    for round_index in range(ROUNDS):
        pattern = jnp.left_shift(jnp.int32(1), plan[round_index].astype(jnp.int32))
        source_all = sources[round_index].reshape(N_DOM, EDGES)
        target_all = targets[round_index].reshape(N_DOM, EDGES)
        kind_all = relation_ids[round_index].reshape(N_DOM, EDGES)
        negative_all = negatives[round_index].reshape(N_DOM, SPANS, NEG)
        counts = edge_counts[round_index]

        def visit(carry, device):
            grads, rel_total = carry
            partner_id = jnp.bitwise_xor(device, pattern)
            owned_grad, partner_grad, rel_grad = bucket_grads(blocks[device], blocks[partner_id], relations, source_all[device], target_all[device], kind_all[device], negative_all[device], counts[device])
            grads = grads.at[device].add(owned_grad).at[partner_id].add(partner_grad)
            return ((grads, rel_total + rel_grad), None)
        start = (jnp.zeros((N_DOM, ROWS, W), jnp.float32), jnp.zeros((RELS, W), jnp.float32))
        (grads, rel_total), _ = lax.scan(visit, start, jnp.arange(N_DOM, dtype=jnp.int32))
        blocks, states = adagrad(blocks, states, grads)
        relations, rel_state = adagrad(relations, rel_state, rel_total)
    return (blocks.reshape(N_DOM * ROWS, W), states.reshape(N_DOM * ROWS), relations, rel_state)
```

```python
from functools import partial

import jax
import jax.numpy as jnp
from jax import lax
from jax.experimental import pallas as pl
from jax.experimental.pallas import tpu as pltpu
from jax.sharding import PartitionSpec as P

NEG = 512
ROUNDS = 3
BITS = 5
WIDTH = 256
RELS = 256
HALF = RELS // 2
PIECE = 8

learn_rate = 0.1
highest = lax.Precision.HIGHEST


def swapped(blocks, bit_number):
    route = []
    for low in range(lax.axis_size("dom")):
        route.append((low, low ^ (1 << bit_number)))
    return tuple(lax.ppermute(block, "dom", route) for block in blocks)


def by_partner(blocks, which):
    branches = [partial(swapped, bit_number=number) for number in range(BITS)]
    return lax.switch(which, branches, blocks)


def sum_kernel(
    grad_ref,
    total_ref,
    core_in,
    acc,
    plane_in,
    line_in,
    core_sems,
    plane_sems,
    line_sems,
    gather_sems,
    last_sems,
):
    me = lax.axis_index("dom")
    core = me % 2
    y = (me // 2) % 4
    z = (me // 8) % 16
    x = me // 128
    plane = x * 4 + y

    def plane_peer(step):
        other = (plane + step) % 16
        return other, ((other // 4) * 128 + z * 8 + (other % 4) * 2 + core,)

    def line_peer(step):
        return (x * 128 + ((z + step) % 16) * 8 + y * 2 + core,)

    twin = (me + 1 - 2 * core,)

    barrier = pltpu.get_barrier_semaphore()

    def greet(step, carry):
        pl.semaphore_signal(barrier, inc=1, device_id=plane_peer(step)[1], device_id_type=pl.DeviceIdType.MESH)
        pl.semaphore_signal(barrier, inc=1, device_id=line_peer(step), device_id_type=pl.DeviceIdType.MESH)
        return carry

    pl.semaphore_signal(barrier, inc=1, device_id=twin, device_id_type=pl.DeviceIdType.MESH)
    lax.fori_loop(1, 16, greet, 0)
    pl.semaphore_wait(barrier, 31)

    def send(src, dst, sems, slot, device):
        return pltpu.make_async_remote_copy(
            src_ref=src,
            dst_ref=dst,
            send_sem=sems.at[0, slot],
            recv_sem=sems.at[1, slot],
            device_id=device,
            device_id_type=pl.DeviceIdType.MESH,
        )

    def each(make):
        def begin(step, carry):
            make(step).start()
            return carry

        def end(step, carry):
            make(step).wait()
            return carry

        lax.fori_loop(1, 16, begin, 0)
        lax.fori_loop(1, 16, end, 0)

    mine = pl.multiple_of(core * HALF, HALF)
    theirs = pl.multiple_of((1 - core) * HALF, HALF)
    swap = send(grad_ref.at[pl.ds(theirs, HALF)], core_in, core_sems, 0, twin)
    swap.start()
    swap.wait()
    acc[...] = grad_ref[pl.ds(mine, HALF), :] + core_in[...]

    def to_plane(step):
        other, device = plane_peer(step)
        rows = pl.ds(pl.multiple_of(other * PIECE, PIECE), PIECE)
        return send(acc.at[rows], plane_in.at[step], plane_sems, step, device)

    each(to_plane)
    own_rows = pl.ds(pl.multiple_of(plane * PIECE, PIECE), PIECE)
    part = acc[own_rows, :]
    for step in range(1, 16):
        part = part + plane_in[step]
    line_in[z] = part

    def to_line(step):
        return send(line_in.at[z], line_in.at[z], line_sems, step, line_peer(step))

    each(to_line)
    part = line_in[0]
    for step in range(1, 16):
        part = part + line_in[step]
    out_rows = pl.ds(pl.multiple_of(core * HALF + plane * PIECE, PIECE), PIECE)
    total_ref[out_rows, :] = part

    def spread_plane(step):
        return send(total_ref.at[out_rows], total_ref.at[out_rows], gather_sems, step, plane_peer(step)[1])

    each(spread_plane)
    half = pl.ds(mine, HALF)
    last = send(total_ref.at[half], total_ref.at[half], last_sems, 0, twin)
    last.start()
    last.wait()


def all_sum(grad):
    return pl.pallas_call(
        sum_kernel,
        out_shape=jax.ShapeDtypeStruct((RELS, WIDTH), jnp.float32),
        in_specs=[pl.BlockSpec(memory_space=pltpu.VMEM)],
        out_specs=pl.BlockSpec(memory_space=pltpu.VMEM),
        scratch_shapes=[
            pltpu.VMEM((HALF, WIDTH), jnp.float32),
            pltpu.VMEM((HALF, WIDTH), jnp.float32),
            pltpu.VMEM((16, PIECE, WIDTH), jnp.float32),
            pltpu.VMEM((16, PIECE, WIDTH), jnp.float32),
            pltpu.SemaphoreType.DMA((2, 1)),
            pltpu.SemaphoreType.DMA((2, 16)),
            pltpu.SemaphoreType.DMA((2, 16)),
            pltpu.SemaphoreType.DMA((2, 16)),
            pltpu.SemaphoreType.DMA((2, 1)),
        ],
        compiler_params=pltpu.CompilerParams(collective_id=0, has_side_effects=True),
    )(grad)


def adagrad(param, state, grad):
    state_new = state + jnp.mean(grad * grad, axis=-1)
    return (param - learn_rate * grad / jnp.sqrt(state_new)[..., None], state_new)


def local(
    embeddings,
    row_state,
    relations,
    rel_state,
    plan,
    edge_counts,
    sources,
    targets,
    relation_ids,
    negatives,
):
    kinds = jnp.arange(RELS, dtype=jnp.int32)[None, :]
    for r in range(ROUNDS):
        which = plan[r]
        mine = sources[r]
        rows = embeddings[mine]
        source, target_ids, kind_ids, flat_neg, count = by_partner(
            (rows, targets[r], relation_ids[r], negatives[r].reshape(-1), edge_counts[r]), which
        )
        live = (jnp.arange(NEG, dtype=jnp.int32) < count[0]).astype(jnp.float32)[:, None]
        onehot = (kind_ids[:, None] == kinds).astype(jnp.float32)
        rel_rows = jnp.dot(onehot, relations, precision=highest)
        query = source * rel_rows * live
        target = embeddings[target_ids]
        neg_rows = embeddings[flat_neg]
        pos_grad = -jax.nn.sigmoid(-jnp.sum(query * target, axis=-1, keepdims=True))
        scores = lax.dot_general(query, neg_rows, (((1,), (1,)), ((), ())), precision=highest)
        neg_grad = jax.nn.sigmoid(scores) / NEG
        spread = jnp.dot(neg_grad, neg_rows, precision=highest)
        query_grad = (pos_grad * target + spread) * live
        negrow_grad = lax.dot_general(neg_grad, query, (((0,), (0,)), ((), ())), precision=highest)
        (back,) = by_partner((query_grad * rel_rows,), which)
        rel_grad = lax.dot_general(onehot, query_grad * source, (((0,), (0,)), ((), ())), precision=highest)
        rel_total = all_sum(rel_grad)
        grads = (
            jnp.zeros(embeddings.shape, jnp.float32)
            .at[target_ids]
            .add(pos_grad * query)
            .at[flat_neg]
            .add(negrow_grad)
            .at[mine]
            .add(back)
        )
        embeddings, row_state = adagrad(embeddings, row_state, grads)
        relations, rel_state = adagrad(relations, rel_state, rel_total)
    return (embeddings, row_state, relations, rel_state)


def solution(mesh):
    placed = (
        P("dom", None),
        P("dom"),
        P(),
        P(),
        P(),
        P(None, "dom"),
        P(None, "dom"),
        P(None, "dom"),
        P(None, "dom"),
        P(None, "dom", None),
    )
    return jax.shard_map(
        local,
        mesh=mesh,
        in_specs=placed,
        out_specs=(P("dom", None), P("dom"), P(), P()),
        check_vma=False,
    )
```

```python
from functools import partial

import jax
import jax.numpy as jnp
from jax import lax
from jax.experimental import pallas as pl
from jax.experimental.pallas import tpu as pltpu
from jax.sharding import PartitionSpec as P

ROUNDS = 3
BITS = 5
WIDTH = 256
RELS = 256
ROWS = 1024
SLOTS = 512
CHUNK = 128
CHUNKS = SLOTS // CHUNK
HALF = RELS // 2
PIECE = 8
SRC, TGT, NEG, REL = 0, 1, 2, 3

learn_rate = 0.1
f32 = jnp.float32
bf16 = jnp.bfloat16


def halves(value):
    high = value.astype(bf16)
    low = (value - high.astype(f32)).astype(bf16)
    return high, low


def pair(value):
    return jnp.concatenate(halves(value), axis=1)


def both(product):
    width = product.shape[1] // 2
    return product[:, :width] + product[:, width:]


def dot(a, b):
    return jnp.dot(a, b, preferred_element_type=f32)


def down(row):
    return jnp.transpose(jnp.broadcast_to(row, (CHUNK, CHUNK)))


def pick(ids_ref, kind, chunk, count):
    column = down(ids_ref[kind : kind + 1, chunk * CHUNK : (chunk + 1) * CHUNK])
    wide = jnp.concatenate([column] * (count // CHUNK), axis=1)
    hit = wide == lax.broadcasted_iota(jnp.int32, (CHUNK, count), 1)
    return jnp.where(hit, 1.0, 0.0).astype(bf16)


def drop(ids_ref, kind, first, count):
    ids = jnp.broadcast_to(ids_ref[kind : kind + 1, :], (count, SLOTS))
    hit = ids == lax.broadcasted_iota(jnp.int32, (count, SLOTS), 0) + first
    return jnp.where(hit, 1.0, 0.0).astype(bf16)


def step(param, state, grad):
    wide = state + jnp.broadcast_to(jnp.mean(grad * grad, axis=1, keepdims=True), state.shape)
    rate = learn_rate * lax.rsqrt(wide)
    return param - grad * jnp.concatenate([rate, rate], axis=1), wide


def round_kernel(
    bit,
    e_ref,
    s_ref,
    r_ref,
    q_ref,
    ids_ref,
    e_out,
    s_out,
    r_out,
    q_out,
    other_ids,
    src_out,
    src_in,
    back_out,
    back_in,
    e_pair,
    target,
    neg_pair,
    rel_rows,
    neg_grad,
    query_pair,
    tgrad_pair,
    rel_pair,
    grad,
    rel_grad,
    core_in,
    acc,
    plane_in,
    line_in,
    total,
    ids_sems,
    src_sems,
    back_sems,
    core_sems,
    plane_sems,
    line_sems,
    gather_sems,
    last_sems,
):
    me = lax.axis_index("dom")
    core = me % 2
    y = (me // 2) % 4
    z = (me // 8) % 16
    x = me // 128
    plane = x * 4 + y
    distance = 1 << bit
    partner = (me + distance - 2 * distance * ((me // distance) % 2),)
    twin = (me + 1 - 2 * core,)

    def plane_peer(hop):
        other = (plane + hop) % 16
        return other, ((other // 4) * 128 + z * 8 + (other % 4) * 2 + core,)

    def line_peer(hop):
        return (x * 128 + ((z + hop) % 16) * 8 + y * 2 + core,)

    barrier = pltpu.get_barrier_semaphore()

    def hail(device):
        pl.semaphore_signal(barrier, inc=1, device_id=device, device_id_type=pl.DeviceIdType.MESH)

    def greet(hop, carry):
        hail(line_peer((hop + 7) % 15 + 1))
        hail(plane_peer(hop)[1])
        return carry

    hail(twin)
    lax.fori_loop(1, 16, greet, 0)

    def send(src, dst, sems, slot, device):
        return pltpu.make_async_remote_copy(
            src_ref=src,
            dst_ref=dst,
            send_sem=sems.at[0, slot],
            recv_sem=sems.at[1, slot],
            device_id=device,
            device_id_type=pl.DeviceIdType.MESH,
        )

    def begin(make):
        def go(hop, carry):
            make(hop).start()
            return carry

        lax.fori_loop(1, 16, go, 0)

    def finish(make):
        def go(hop, carry):
            make(hop).wait()
            return carry

        lax.fori_loop(1, 16, go, 0)

    def part(chunk):
        return pl.ds(chunk * CHUNK, CHUNK)

    e_pair[...] = pair(e_ref[...])
    for c in range(CHUNKS):
        src_out[part(c), :] = both(dot(pick(ids_ref, SRC, c, ROWS), e_pair[...]))

    pl.semaphore_wait(barrier, 31)
    ids_copy = send(ids_ref, other_ids, ids_sems, 0, partner)
    ids_copy.start()
    src_copies = [send(src_out.at[part(c)], src_in.at[part(c)], src_sems, c, partner) for c in range(CHUNKS)]
    for copy in src_copies:
        copy.start()
    ids_copy.wait()

    relations = pair(r_ref[...])
    for c in range(CHUNKS):
        target[part(c), :] = both(dot(pick(other_ids, TGT, c, ROWS), e_pair[...]))
        neg_pair[part(c), :] = dot(pick(other_ids, NEG, c, ROWS), e_pair[...]).astype(bf16)
        rel_rows[part(c), :] = both(dot(pick(other_ids, REL, c, RELS), relations))

    back_copies = []
    for c in range(CHUNKS):
        src_copies[c].wait()
        source = src_in[part(c), :]
        kinds = rel_rows[part(c), :]
        towards = target[part(c), :]
        query = source * kinds
        pos_grad = -jax.nn.sigmoid(-jnp.sum(query * towards, axis=1, keepdims=True))
        q_high, q_low = halves(query)
        n_high, n_low = neg_pair[:, :WIDTH], neg_pair[:, WIDTH:]
        across = (((1,), (1,)), ((), ()))
        scores = (
            lax.dot_general(q_high, n_high, across, preferred_element_type=f32)
            + lax.dot_general(q_high, n_low, across, preferred_element_type=f32)
            + lax.dot_general(q_low, n_high, across, preferred_element_type=f32)
        )
        pushes = jax.nn.sigmoid(scores) * (1.0 / SLOTS)
        neg_grad[part(c), :] = pushes
        p_high, p_low = halves(pushes)
        spread = both(dot(p_high, neg_pair[...])) + dot(p_low, n_high)
        query_grad = pos_grad * towards + spread
        back_out[part(c), :] = query_grad * kinds
        copy = send(back_out.at[part(c)], back_in.at[part(c)], back_sems, c, partner)
        copy.start()
        back_copies.append(copy)
        query_pair[part(c), :WIDTH] = q_high
        query_pair[part(c), WIDTH:] = q_low
        tgrad_pair[part(c), :] = pair(pos_grad * query)
        rel_pair[part(c), :] = pair(query_grad * source)

    rel_grad[...] = both(dot(drop(other_ids, REL, 0, RELS), rel_pair[...]))
    mine = pl.multiple_of(core * HALF, HALF)
    theirs = pl.multiple_of((1 - core) * HALF, HALF)
    swap = send(rel_grad.at[pl.ds(theirs, HALF)], core_in, core_sems, 0, twin)
    swap.start()

    turned = jnp.transpose(neg_grad[...])
    t_high, t_low = halves(turned)
    negrow = pair(both(dot(t_high, query_pair[...])) + dot(t_low, query_pair[:, :WIDTH]))

    swap.wait()
    acc[...] = rel_grad[pl.ds(mine, HALF), :] + core_in[...]

    def to_plane(hop):
        other, device = plane_peer(hop)
        rows = pl.ds(pl.multiple_of(other * PIECE, PIECE), PIECE)
        return send(acc.at[rows], plane_in.at[hop], plane_sems, hop, device)

    begin(to_plane)
    for b in range(ROWS // HALF):
        rows = pl.ds(b * HALF, HALF)
        grad[rows, :] = both(
            dot(drop(other_ids, TGT, b * HALF, HALF), tgrad_pair[...])
            + dot(drop(other_ids, NEG, b * HALF, HALF), negrow)
        )
    finish(to_plane)
    own = acc[pl.ds(pl.multiple_of(plane * PIECE, PIECE), PIECE), :]
    for hop in range(1, 16):
        own = own + plane_in[hop]
    line_in[z] = own

    def to_line(hop):
        far = (hop + 7) % 15 + 1
        return send(line_in.at[z], line_in.at[z], line_sems, far, line_peer(far))

    begin(to_line)
    finish(to_line)
    own = line_in[0]
    for hop in range(1, 16):
        own = own + line_in[hop]
    own_rows = pl.ds(pl.multiple_of(core * HALF + plane * PIECE, PIECE), PIECE)
    total[own_rows, :] = own

    def spread_plane(hop):
        return send(total.at[own_rows], total.at[own_rows], gather_sems, hop, plane_peer(hop)[1])

    begin(spread_plane)
    finish(spread_plane)
    half = pl.ds(mine, HALF)
    last = send(total.at[half], total.at[half], last_sems, 0, twin)
    last.start()

    for copy in back_copies:
        copy.wait()
    back = pair(back_in[...])
    for b in range(ROWS // CHUNK):
        rows = part(b)
        whole = grad[rows, :] + both(dot(drop(ids_ref, SRC, b * CHUNK, CHUNK), back))
        fresh, wide = step(e_ref[rows, :], down(s_ref[b : b + 1, :]), whole)
        e_out[rows, :] = fresh
        s_out[b : b + 1, :] = jnp.transpose(wide)[0:1, :]

    last.wait()
    for b in range(RELS // CHUNK):
        rows = part(b)
        fresh, wide = step(r_ref[rows, :], down(q_ref[b : b + 1, :]), total[rows, :])
        r_out[rows, :] = fresh
        q_out[b : b + 1, :] = jnp.transpose(wide)[0:1, :]


def run_round(state, bit):
    vmem = pl.BlockSpec(memory_space=pltpu.VMEM)
    sems = [pltpu.SemaphoreType.DMA((2, n)) for n in (1, CHUNKS, CHUNKS, 1, 16, 16, 16, 1)]
    return tuple(
        pl.pallas_call(
            partial(round_kernel, bit),
            out_shape=tuple(jax.ShapeDtypeStruct(a.shape, a.dtype) for a in state[:4]),
            in_specs=[vmem] * 5,
            out_specs=(vmem,) * 4,
            scratch_shapes=[
                pltpu.VMEM((8, SLOTS), jnp.int32),
                pltpu.VMEM((SLOTS, WIDTH), f32),
                pltpu.VMEM((SLOTS, WIDTH), f32),
                pltpu.VMEM((SLOTS, WIDTH), f32),
                pltpu.VMEM((SLOTS, WIDTH), f32),
                pltpu.VMEM((ROWS, 2 * WIDTH), bf16),
                pltpu.VMEM((SLOTS, WIDTH), f32),
                pltpu.VMEM((SLOTS, 2 * WIDTH), bf16),
                pltpu.VMEM((SLOTS, WIDTH), f32),
                pltpu.VMEM((SLOTS, SLOTS), f32),
                pltpu.VMEM((SLOTS, 2 * WIDTH), bf16),
                pltpu.VMEM((SLOTS, 2 * WIDTH), bf16),
                pltpu.VMEM((SLOTS, 2 * WIDTH), bf16),
                pltpu.VMEM((ROWS, WIDTH), f32),
                pltpu.VMEM((RELS, WIDTH), f32),
                pltpu.VMEM((HALF, WIDTH), f32),
                pltpu.VMEM((HALF, WIDTH), f32),
                pltpu.VMEM((16, PIECE, WIDTH), f32),
                pltpu.VMEM((16, PIECE, WIDTH), f32),
                pltpu.VMEM((RELS, WIDTH), f32),
                *sems,
            ],
            compiler_params=pltpu.CompilerParams(
                collective_id=bit, has_side_effects=True, vmem_limit_bytes=48 * 1024 * 1024
            ),
        )(*state)
    )


def local(
    embeddings,
    row_state,
    relations,
    rel_state,
    plan,
    edge_counts,
    sources,
    targets,
    relation_ids,
    negatives,
):
    live = jnp.arange(SLOTS, dtype=jnp.int32)[None, :] < edge_counts
    kinds = jnp.where(live, relation_ids, -1)
    ids = jnp.stack([sources, targets, negatives.reshape(ROUNDS, SLOTS), kinds] * 2, axis=1)
    state = (embeddings, row_state.reshape(-1, CHUNK), relations, rel_state.reshape(-1, CHUNK))
    branches = [partial(run_round, bit=bit) for bit in range(BITS)]
    for r in range(ROUNDS):
        state = lax.switch(plan[r], branches, (*state, ids[r]))
    embeddings, row_state, relations, rel_state = state
    return (embeddings, row_state.reshape(-1), relations, rel_state.reshape(-1))


def solution(mesh):
    placed = (
        P("dom", None),
        P("dom"),
        P(),
        P(),
        P(),
        P(None, "dom"),
        P(None, "dom"),
        P(None, "dom"),
        P(None, "dom"),
        P(None, "dom", None),
    )
    return jax.shard_map(
        local,
        mesh=mesh,
        in_specs=placed,
        out_specs=(P("dom", None), P("dom"), P(), P()),
        check_vma=False,
    )
```

```python
from functools import partial

import jax
import jax.numpy as jnp
from jax import lax
from jax.experimental import pallas as pl
from jax.experimental.pallas import tpu as pltpu
from jax.sharding import PartitionSpec as P

ROUNDS = 3
BITS = 5
WIDTH = 256
RELS = 256
ROWS = 1024
SLOTS = 512
CHUNK = 128
CHUNKS = SLOTS // CHUNK
HALF = RELS // 2
PIECE = 8
SRC, TGT, NEG, REL = 0, 1, 2, 3

learn_rate = 0.1
f32 = jnp.float32
bf16 = jnp.bfloat16


def halves(value):
    high = value.astype(bf16)
    low = (value - high.astype(f32)).astype(bf16)
    return high, low


def pair(value):
    return jnp.concatenate(halves(value), axis=1)


def both(product):
    width = product.shape[1] // 2
    return product[:, :width] + product[:, width:]


def dot(a, b):
    return jnp.dot(a, b, preferred_element_type=f32)


def down(row):
    return jnp.transpose(jnp.broadcast_to(row, (CHUNK, CHUNK)))


def pick(ids, row, count):
    column = down(ids[pl.ds(row, 1), :])
    wide = jnp.concatenate([column] * (count // CHUNK), axis=1)
    hit = wide == lax.broadcasted_iota(jnp.int32, (CHUNK, count), 1)
    return jnp.where(hit, 1.0, 0.0).astype(bf16)


def drop(ids, kind, first, count):
    rows = [ids[kind * CHUNKS + c : kind * CHUNKS + c + 1, :] for c in range(CHUNKS)]
    wide = jnp.broadcast_to(jnp.concatenate(rows, axis=1), (count, SLOTS))
    hit = wide == lax.broadcasted_iota(jnp.int32, (count, SLOTS), 0) + first
    return jnp.where(hit, 1.0, 0.0).astype(bf16)


def loop(count, body):
    def go(index, carry):
        body(index)
        return carry

    lax.fori_loop(0, count, go, 0)


def step(param, state, grad):
    wide = state + jnp.broadcast_to(jnp.mean(grad * grad, axis=1, keepdims=True), state.shape)
    rate = learn_rate * lax.rsqrt(wide)
    return param - grad * jnp.concatenate([rate, rate], axis=1), wide


def round_kernel(
    bit,
    e_ref,
    s_ref,
    r_ref,
    q_ref,
    ids_ref,
    others_ref,
    e_out,
    s_out,
    r_out,
    q_out,
    ids_now,
    src_in,
    back_out,
    back_in,
    e_pair,
    taken,
    taken_pair,
    rel_rows,
    r_pair,
    neg_grad,
    negrow_pair,
    back_pair,
    query_pair,
    tgrad_pair,
    rel_pair,
    grad,
    rel_grad,
    core_in,
    acc,
    plane_in,
    line_in,
    total,
    src_sems,
    back_sems,
    core_sems,
    plane_sems,
    line_sems,
    gather_sems,
    last_sems,
):
    me = lax.axis_index("dom")
    core = me % 2
    y = (me // 2) % 4
    z = (me // 8) % 16
    x = me // 128
    plane = x * 4 + y
    distance = 1 << bit
    partner = (me + distance - 2 * distance * ((me // distance) % 2),)
    twin = (me + 1 - 2 * core,)

    def plane_peer(hop):
        other = (plane + hop) % 16
        return other, ((other // 4) * 128 + z * 8 + (other % 4) * 2 + core,)

    def line_peer(hop):
        return (x * 128 + ((z + hop) % 16) * 8 + y * 2 + core,)

    barrier = pltpu.get_barrier_semaphore()

    def hail(device):
        pl.semaphore_signal(barrier, inc=1, device_id=device, device_id_type=pl.DeviceIdType.MESH)

    def greet(hop, carry):
        hail(line_peer((hop + 7) % 15 + 1))
        hail(plane_peer(hop)[1])
        return carry

    hail(twin)
    lax.fori_loop(1, 16, greet, 0)

    def send(src, dst, sems, slot, device):
        return pltpu.make_async_remote_copy(
            src_ref=src,
            dst_ref=dst,
            send_sem=sems.at[0, slot],
            recv_sem=sems.at[1, slot],
            device_id=device,
            device_id_type=pl.DeviceIdType.MESH,
        )

    def begin(make):
        def go(hop, carry):
            make(hop).start()
            return carry

        lax.fori_loop(1, 16, go, 0)

    def finish(make):
        def go(hop, carry):
            make(hop).wait()
            return carry

        lax.fori_loop(1, 16, go, 0)

    def part(chunk):
        return pl.ds(pl.multiple_of(chunk * CHUNK, CHUNK), CHUNK)

    def source_copy(c):
        return send(taken.at[part(c)], src_in.at[part(c)], src_sems, c, partner)

    def back_copy(c):
        return send(back_out.at[part(c)], back_in.at[part(c)], back_sems, c, partner)

    other_ids = others_ref.at[bit]
    ids_now[...] = jnp.where(
        lax.broadcasted_iota(jnp.int32, (4 * CHUNKS, CHUNK), 0) < CHUNKS, ids_ref[...], other_ids[...]
    )

    def split_rows(b):
        e_pair[part(b), :] = pair(e_ref[part(b), :])

    loop(ROWS // CHUNK, split_rows)
    r_pair[...] = pair(r_ref[...])

    def take(i):
        found = dot(pick(ids_now, i, ROWS), e_pair[...])
        taken[part(i), :] = both(found)
        taken_pair[part(i), :] = found.astype(bf16)

    loop(3 * CHUNKS, take)

    def take_relations(c):
        rel_rows[part(c), :] = both(dot(pick(ids_now, REL * CHUNKS + c, RELS), r_pair[...]))

    loop(CHUNKS, take_relations)
    pl.semaphore_wait(barrier, 31)
    loop(CHUNKS, lambda c: source_copy(c).start())
    neg_pair = taken_pair.at[pl.ds(NEG * SLOTS, SLOTS)]

    early = (0, 0, 0, 3, 2)[bit]

    def score(c):
        source_copy(c).wait()
        source = src_in[part(c), :]
        kinds = rel_rows[part(c), :]
        towards = taken[part(TGT * CHUNKS + c), :]
        query = source * kinds
        pos_grad = -jax.nn.sigmoid(-jnp.sum(query * towards, axis=1, keepdims=True))
        q_high, q_low = halves(query)
        n_high, n_low = neg_pair[:, :WIDTH], neg_pair[:, WIDTH:]
        across = (((1,), (1,)), ((), ()))
        scores = (
            lax.dot_general(q_high, n_high, across, preferred_element_type=f32)
            + lax.dot_general(q_high, n_low, across, preferred_element_type=f32)
            + lax.dot_general(q_low, n_high, across, preferred_element_type=f32)
        )
        pushes = jax.nn.sigmoid(scores) * (1.0 / SLOTS)
        for k in range(CHUNKS):
            neg_grad[k, part(c), :] = pushes[:, k * CHUNK : (k + 1) * CHUNK]
        p_high, p_low = halves(pushes)
        spread = both(dot(p_high, neg_pair[...])) + dot(p_low, n_high)
        query_grad = pos_grad * towards + spread
        back_out[part(c), :] = query_grad * kinds
        query_pair[part(c), :WIDTH] = q_high
        query_pair[part(c), WIDTH:] = q_low
        tgrad_pair[part(c), :] = pair(pos_grad * query)
        rel_pair[part(c), :] = pair(query_grad * source)

    def score_and_send(c):
        score(c)

        @pl.when(c < early)
        def _():
            back_copy(c).start()

    loop(CHUNKS, score_and_send if early else score)

    def send_rest():
        for c in range(early, CHUNKS):
            back_copy(c).start()

    rel_grad[...] = both(dot(drop(other_ids, REL, 0, RELS), rel_pair[...]))
    mine = pl.multiple_of(core * HALF, HALF)
    theirs = pl.multiple_of((1 - core) * HALF, HALF)
    swap = send(rel_grad.at[pl.ds(theirs, HALF)], core_in, core_sems, 0, twin)
    swap.start()

    def turn(k):
        t_high, t_low = halves(jnp.transpose(neg_grad[k]))
        negrow = both(dot(t_high, query_pair[...])) + dot(t_low, query_pair[:, :WIDTH])
        negrow_pair[part(k), :] = pair(negrow)

    loop(CHUNKS, turn)

    swap.wait()
    acc[...] = rel_grad[pl.ds(mine, HALF), :] + core_in[...]

    def to_plane(hop):
        other, device = plane_peer(hop)
        rows = pl.ds(pl.multiple_of(other * PIECE, PIECE), PIECE)
        return send(acc.at[rows], plane_in.at[hop], plane_sems, hop, device)

    begin(to_plane)
    if bit < 3:
        send_rest()

    def scatter(b):
        grad[part(b), :] = both(
            dot(drop(other_ids, TGT, b * CHUNK, CHUNK), tgrad_pair[...])
            + dot(drop(other_ids, NEG, b * CHUNK, CHUNK), negrow_pair[...])
        )

    loop(ROWS // CHUNK, scatter)
    finish(to_plane)
    own = acc[pl.ds(pl.multiple_of(plane * PIECE, PIECE), PIECE), :]
    for hop in range(1, 16):
        own = own + plane_in[hop]
    line_in[z] = own

    def to_line(hop):
        far = (hop + 7) % 15 + 1
        return send(line_in.at[z], line_in.at[z], line_sems, far, line_peer(far))

    def update_entities():
        def land(c):
            back_copy(c).wait()
            back_pair[part(c), :] = pair(back_in[part(c), :])

        loop(CHUNKS, land)

        def update(b):
            whole = grad[part(b), :] + both(dot(drop(ids_ref, SRC, b * CHUNK, CHUNK), back_pair[...]))
            fresh, wide = step(e_ref[part(b), :], down(s_ref[pl.ds(b, 1), :]), whole)
            e_out[part(b), :] = fresh
            s_out[pl.ds(b, 1), :] = jnp.transpose(wide)[0:1, :]

        loop(ROWS // CHUNK, update)

    begin(to_line)
    if bit >= 3:
        send_rest()
    if bit < 4:
        update_entities()
    finish(to_line)
    own = line_in[0]
    for hop in range(1, 16):
        own = own + line_in[hop]
    own_rows = pl.ds(pl.multiple_of(core * HALF + plane * PIECE, PIECE), PIECE)
    total[own_rows, :] = own

    def spread_plane(hop):
        return send(total.at[own_rows], total.at[own_rows], gather_sems, hop, plane_peer(hop)[1])

    begin(spread_plane)
    finish(spread_plane)
    half = pl.ds(mine, HALF)
    last = send(total.at[half], total.at[half], last_sems, 0, twin)
    last.start()

    if bit == 4:
        update_entities()
    last.wait()

    def update_relations(b):
        fresh, wide = step(r_ref[part(b), :], down(q_ref[pl.ds(b, 1), :]), total[part(b), :])
        r_out[part(b), :] = fresh
        q_out[pl.ds(b, 1), :] = jnp.transpose(wide)[0:1, :]

    loop(RELS // CHUNK, update_relations)


def run_round(state, bit):
    vmem = pl.BlockSpec(memory_space=pltpu.VMEM)
    sems = [pltpu.SemaphoreType.DMA((2, n)) for n in (CHUNKS, CHUNKS, 1, 16, 16, 16, 1)]
    return tuple(
        pl.pallas_call(
            partial(round_kernel, bit),
            out_shape=tuple(jax.ShapeDtypeStruct(a.shape, a.dtype) for a in state[:4]),
            in_specs=[vmem] * 6,
            out_specs=(vmem,) * 4,
            scratch_shapes=[
                pltpu.VMEM((4 * CHUNKS, CHUNK), jnp.int32),
                pltpu.VMEM((SLOTS, WIDTH), f32),
                pltpu.VMEM((SLOTS, WIDTH), f32),
                pltpu.VMEM((SLOTS, WIDTH), f32),
                pltpu.VMEM((ROWS, 2 * WIDTH), bf16),
                pltpu.VMEM((3 * SLOTS, WIDTH), f32),
                pltpu.VMEM((3 * SLOTS, 2 * WIDTH), bf16),
                pltpu.VMEM((SLOTS, WIDTH), f32),
                pltpu.VMEM((RELS, 2 * WIDTH), bf16),
                pltpu.VMEM((CHUNKS, SLOTS, CHUNK), f32),
                pltpu.VMEM((SLOTS, 2 * WIDTH), bf16),
                pltpu.VMEM((SLOTS, 2 * WIDTH), bf16),
                pltpu.VMEM((SLOTS, 2 * WIDTH), bf16),
                pltpu.VMEM((SLOTS, 2 * WIDTH), bf16),
                pltpu.VMEM((SLOTS, 2 * WIDTH), bf16),
                pltpu.VMEM((ROWS, WIDTH), f32),
                pltpu.VMEM((RELS, WIDTH), f32),
                pltpu.VMEM((HALF, WIDTH), f32),
                pltpu.VMEM((HALF, WIDTH), f32),
                pltpu.VMEM((16, PIECE, WIDTH), f32),
                pltpu.VMEM((16, PIECE, WIDTH), f32),
                pltpu.VMEM((RELS, WIDTH), f32),
                *sems,
            ],
            compiler_params=pltpu.CompilerParams(
                collective_id=bit, has_side_effects=True, vmem_limit_bytes=48 * 1024 * 1024
            ),
        )(*state)
    )


def ids_kernel(counts_ref, src_ref, tgt_ref, rel_ref, neg_ref, *rest):
    own, others, sems = rest[:ROUNDS], rest[ROUNDS : 2 * ROUNDS], rest[2 * ROUNDS]
    me = lax.axis_index("dom")
    partners = []
    for bit in range(BITS):
        distance = 1 << bit
        partners.append((me + distance - 2 * distance * ((me // distance) % 2),))
    barrier = pltpu.get_barrier_semaphore()
    for partner in partners:
        pl.semaphore_signal(barrier, inc=1, device_id=partner, device_id_type=pl.DeviceIdType.MESH)
    for r in range(ROUNDS):
        for c in range(CHUNKS):
            lanes = slice(c * CHUNK, (c + 1) * CHUNK)
            slots = lax.broadcasted_iota(jnp.int32, (1, CHUNK), 1) + c * CHUNK
            kinds = jnp.where(slots < counts_ref[r : r + 1, :], rel_ref[r : r + 1, lanes], -1)
            own[r][SRC * CHUNKS + c : SRC * CHUNKS + c + 1, :] = src_ref[r : r + 1, lanes]
            own[r][TGT * CHUNKS + c : TGT * CHUNKS + c + 1, :] = tgt_ref[r : r + 1, lanes]
            own[r][NEG * CHUNKS + c : NEG * CHUNKS + c + 1, :] = neg_ref[r, :, lanes]
            own[r][REL * CHUNKS + c : REL * CHUNKS + c + 1, :] = kinds
    pl.semaphore_wait(barrier, BITS)
    copies = []
    for r in range(ROUNDS):
        for bit in range(BITS):
            copies.append(
                pltpu.make_async_remote_copy(
                    src_ref=own[r],
                    dst_ref=others[r].at[bit],
                    send_sem=sems.at[0, r * BITS + bit],
                    recv_sem=sems.at[1, r * BITS + bit],
                    device_id=partners[bit],
                    device_id_type=pl.DeviceIdType.MESH,
                )
            )
    for copy in copies:
        copy.start()
    for copy in copies:
        copy.wait()


def trade_ids(*arrays):
    vmem = pl.BlockSpec(memory_space=pltpu.VMEM)
    own = [jax.ShapeDtypeStruct((4 * CHUNKS, CHUNK), jnp.int32)] * ROUNDS
    others = [jax.ShapeDtypeStruct((BITS, 4 * CHUNKS, CHUNK), jnp.int32)] * ROUNDS
    made = pl.pallas_call(
        ids_kernel,
        out_shape=(*own, *others),
        in_specs=[vmem] * len(arrays),
        out_specs=(vmem,) * (2 * ROUNDS),
        scratch_shapes=[pltpu.SemaphoreType.DMA((2, ROUNDS * BITS))],
        compiler_params=pltpu.CompilerParams(collective_id=BITS, has_side_effects=True),
    )(*arrays)
    return made[:ROUNDS], made[ROUNDS:]


def local(
    embeddings,
    row_state,
    relations,
    rel_state,
    plan,
    edge_counts,
    sources,
    targets,
    relation_ids,
    negatives,
):
    own, others = trade_ids(edge_counts, sources, targets, relation_ids, negatives)
    state = (embeddings, row_state.reshape(-1, CHUNK), relations, rel_state.reshape(-1, CHUNK))
    branches = [partial(run_round, bit=bit) for bit in range(BITS)]
    for r in range(ROUNDS):
        state = lax.switch(plan[r], branches, (*state, own[r], others[r]))
    embeddings, row_state, relations, rel_state = state
    return (embeddings, row_state.reshape(-1), relations, rel_state.reshape(-1))


def solution(mesh):
    placed = (
        P("dom", None),
        P("dom"),
        P(),
        P(),
        P(),
        P(None, "dom"),
        P(None, "dom"),
        P(None, "dom"),
        P(None, "dom"),
        P(None, "dom", None),
    )
    return jax.shard_map(
        local,
        mesh=mesh,
        in_specs=placed,
        out_specs=(P("dom", None), P("dom"), P(), P()),
        check_vma=False,
    )
```

```python
from functools import partial

import jax
import jax.numpy as jnp
from jax import lax
from jax.experimental import pallas as pl
from jax.experimental.pallas import tpu as pltpu
from jax.sharding import PartitionSpec as P

ROUNDS = 3
BITS = 5
WIDTH = 256
RELS = 256
ROWS = 1024
SLOTS = 512
CHUNK = 128
CHUNKS = SLOTS // CHUNK
HALF = RELS // 2
PIECE = 8
SRC, TGT, NEG, REL = 0, 1, 2, 3

learn_rate = 0.1
f32 = jnp.float32
bf16 = jnp.bfloat16


def halves(value):
    high = value.astype(bf16)
    low = (value - high.astype(f32)).astype(bf16)
    return high, low


def pair(value):
    return jnp.concatenate(halves(value), axis=1)


def both(product):
    width = product.shape[1] // 2
    return product[:, :width] + product[:, width:]


def dot(a, b):
    return jnp.dot(a, b, preferred_element_type=f32)


def down(row):
    return jnp.transpose(jnp.broadcast_to(row, (CHUNK, CHUNK)))


def pick(ids, row, count):
    column = down(ids[pl.ds(row, 1), :])
    wide = jnp.concatenate([column] * (count // CHUNK), axis=1)
    hit = wide == lax.broadcasted_iota(jnp.int32, (CHUNK, count), 1)
    return jnp.where(hit, 1.0, 0.0).astype(bf16)


def drop(ids, kind, first, count):
    rows = [ids[kind * CHUNKS + c : kind * CHUNKS + c + 1, :] for c in range(CHUNKS)]
    wide = jnp.broadcast_to(jnp.concatenate(rows, axis=1), (count, SLOTS))
    hit = wide == lax.broadcasted_iota(jnp.int32, (count, SLOTS), 0) + first
    return jnp.where(hit, 1.0, 0.0).astype(bf16)


def loop(count, body):
    def go(index, carry):
        body(index)
        return carry

    lax.fori_loop(0, count, go, 0)


def step(param, state, grad):
    wide = state + jnp.broadcast_to(jnp.mean(grad * grad, axis=1, keepdims=True), state.shape)
    rate = learn_rate * lax.rsqrt(wide)
    return param - grad * jnp.concatenate([rate, rate], axis=1), wide


def round_kernel(
    bit,
    e_ref,
    s_ref,
    r_ref,
    q_ref,
    ids_ref,
    others_ref,
    e_out,
    s_out,
    r_out,
    q_out,
    ids_now,
    src_in,
    back_out,
    back_in,
    e_pair,
    taken,
    taken_pair,
    rel_hits,
    rel_rows,
    r_pair,
    neg_grad,
    negrow_pair,
    back_pair,
    query_pair,
    tgrad_pair,
    rel_pair,
    grad,
    rel_grad,
    core_in,
    acc,
    plane_in,
    line_in,
    total,
    src_sems,
    back_sems,
    core_sems,
    plane_sems,
    line_sems,
    gather_sems,
    last_sems,
):
    me = lax.axis_index("dom")
    core = me % 2
    y = (me // 2) % 4
    z = (me // 8) % 16
    x = me // 128
    plane = x * 4 + y
    distance = 1 << bit
    partner = (me + distance - 2 * distance * ((me // distance) % 2),)
    twin = (me + 1 - 2 * core,)

    def plane_peer(hop):
        other = (plane + hop) % 16
        return other, ((other // 4) * 128 + z * 8 + (other % 4) * 2 + core,)

    def line_peer(hop):
        return (x * 128 + ((z + hop) % 16) * 8 + y * 2 + core,)

    barrier = pltpu.get_barrier_semaphore()

    def hail(device):
        pl.semaphore_signal(barrier, inc=1, device_id=device, device_id_type=pl.DeviceIdType.MESH)

    def greet(hop, carry):
        hail(line_peer((hop + 7) % 15 + 1))
        hail(plane_peer(hop)[1])
        return carry

    hail(twin)
    lax.fori_loop(1, 16, greet, 0)

    def send(src, dst, sems, slot, device):
        return pltpu.make_async_remote_copy(
            src_ref=src,
            dst_ref=dst,
            send_sem=sems.at[0, slot],
            recv_sem=sems.at[1, slot],
            device_id=device,
            device_id_type=pl.DeviceIdType.MESH,
        )

    def begin(make):
        def go(hop, carry):
            make(hop).start()
            return carry

        lax.fori_loop(1, 16, go, 0)

    def finish(make):
        def go(hop, carry):
            make(hop).wait()
            return carry

        lax.fori_loop(1, 16, go, 0)

    def part(chunk):
        return pl.ds(pl.multiple_of(chunk * CHUNK, CHUNK), CHUNK)

    def source_copy(c):
        return send(taken.at[part(c)], src_in.at[part(c)], src_sems, c, partner)

    def back_copy(c):
        return send(back_out.at[part(c)], back_in.at[part(c)], back_sems, c, partner)

    other_ids = others_ref.at[bit]
    ids_now[...] = jnp.where(
        lax.broadcasted_iota(jnp.int32, (4 * CHUNKS, CHUNK), 0) < CHUNKS, ids_ref[...], other_ids[...]
    )

    def split_rows(b):
        e_pair[part(b), :] = pair(e_ref[part(b), :])

    loop(ROWS // CHUNK, split_rows)
    r_pair[...] = pair(r_ref[...])

    def take(i):
        found = dot(pick(ids_now, i, ROWS), e_pair[...])
        taken[part(i), :] = both(found)
        taken_pair[part(i), :] = found.astype(bf16)

    loop(3 * CHUNKS, take)

    def take_relations(c):
        rel_rows[part(c), :] = both(dot(pick(ids_now, REL * CHUNKS + c, RELS), r_pair[...]))

    loop(CHUNKS, take_relations)
    rel_hits[...] = drop(ids_now, REL, 0, RELS)
    pl.semaphore_wait(barrier, 31)
    loop(CHUNKS, lambda c: source_copy(c).start())
    neg_pair = taken_pair.at[pl.ds(NEG * SLOTS, SLOTS)]

    early = (0, 0, 2, 3, 2)[bit]

    def score(c):
        source_copy(c).wait()
        source = src_in[part(c), :]
        kinds = rel_rows[part(c), :]
        towards = taken[part(TGT * CHUNKS + c), :]
        query = source * kinds
        pos_grad = -jax.nn.sigmoid(-jnp.sum(query * towards, axis=1, keepdims=True))
        q_high, q_low = halves(query)
        n_high, n_low = neg_pair[:, :WIDTH], neg_pair[:, WIDTH:]
        across = (((1,), (1,)), ((), ()))
        scores = (
            lax.dot_general(q_high, n_high, across, preferred_element_type=f32)
            + lax.dot_general(q_high, n_low, across, preferred_element_type=f32)
            + lax.dot_general(q_low, n_high, across, preferred_element_type=f32)
        )
        pushes = jax.nn.sigmoid(scores) * (1.0 / SLOTS)
        for k in range(CHUNKS):
            neg_grad[k, part(c), :] = pushes[:, k * CHUNK : (k + 1) * CHUNK]
        p_high, p_low = halves(pushes)
        spread = both(dot(p_high, neg_pair[...])) + dot(p_low, n_high)
        query_grad = pos_grad * towards + spread
        back_out[part(c), :] = query_grad * kinds
        query_pair[part(c), :WIDTH] = q_high
        query_pair[part(c), WIDTH:] = q_low
        tgrad_pair[part(c), :] = pair(pos_grad * query)
        rel_pair[part(c), :] = pair(query_grad * source)

    def score_and_send(c):
        score(c)

        @pl.when(c < early)
        def _():
            back_copy(c).start()

    loop(CHUNKS, score_and_send if early else score)

    def send_rest():
        for c in range(early, CHUNKS):
            back_copy(c).start()

    rel_grad[...] = both(dot(rel_hits[...], rel_pair[...]))
    mine = pl.multiple_of(core * HALF, HALF)
    theirs = pl.multiple_of((1 - core) * HALF, HALF)
    swap = send(rel_grad.at[pl.ds(theirs, HALF)], core_in, core_sems, 0, twin)
    swap.start()

    def turn(k):
        t_high, t_low = halves(jnp.transpose(neg_grad[k]))
        negrow = both(dot(t_high, query_pair[...])) + dot(t_low, query_pair[:, :WIDTH])
        negrow_pair[part(k), :] = pair(negrow)

    swap.wait()
    acc[...] = rel_grad[pl.ds(mine, HALF), :] + core_in[...]

    def to_plane(hop):
        other, device = plane_peer(hop)
        rows = pl.ds(pl.multiple_of(other * PIECE, PIECE), PIECE)
        return send(acc.at[rows], plane_in.at[hop], plane_sems, hop, device)

    begin(to_plane)
    if bit < 3:
        send_rest()

    loop(CHUNKS, turn)

    def scatter(b):
        grad[part(b), :] = both(
            dot(drop(other_ids, TGT, b * CHUNK, CHUNK), tgrad_pair[...])
            + dot(drop(other_ids, NEG, b * CHUNK, CHUNK), negrow_pair[...])
        )

    loop(ROWS // CHUNK, scatter)
    finish(to_plane)
    own = acc[pl.ds(pl.multiple_of(plane * PIECE, PIECE), PIECE), :]
    for hop in range(1, 16):
        own = own + plane_in[hop]
    line_in[z] = own

    def to_line(hop):
        far = (hop + 7) % 15 + 1
        return send(line_in.at[z], line_in.at[z], line_sems, far, line_peer(far))

    def update_entities():
        def land(c):
            back_copy(c).wait()
            back_pair[part(c), :] = pair(back_in[part(c), :])

        loop(CHUNKS, land)

        def update(b):
            whole = grad[part(b), :] + both(dot(drop(ids_ref, SRC, b * CHUNK, CHUNK), back_pair[...]))
            fresh, wide = step(e_ref[part(b), :], down(s_ref[pl.ds(b, 1), :]), whole)
            e_out[part(b), :] = fresh
            s_out[pl.ds(b, 1), :] = jnp.transpose(wide)[0:1, :]

        loop(ROWS // CHUNK, update)

    begin(to_line)
    if bit >= 3:
        send_rest()
    finish(to_line)
    own = line_in[0]
    for hop in range(1, 16):
        own = own + line_in[hop]
    own_rows = pl.ds(pl.multiple_of(core * HALF + plane * PIECE, PIECE), PIECE)
    total[own_rows, :] = own

    def spread_plane(hop):
        return send(total.at[own_rows], total.at[own_rows], gather_sems, hop, plane_peer(hop)[1])

    begin(spread_plane)
    if bit in (0, 1, 3):
        update_entities()
    finish(spread_plane)
    half = pl.ds(mine, HALF)
    last = send(total.at[half], total.at[half], last_sems, 0, twin)
    last.start()

    if bit in (2, 4):
        update_entities()
    last.wait()

    def update_relations(b):
        fresh, wide = step(r_ref[part(b), :], down(q_ref[pl.ds(b, 1), :]), total[part(b), :])
        r_out[part(b), :] = fresh
        q_out[pl.ds(b, 1), :] = jnp.transpose(wide)[0:1, :]

    loop(RELS // CHUNK, update_relations)


def run_round(state, bit):
    vmem = pl.BlockSpec(memory_space=pltpu.VMEM)
    sems = [pltpu.SemaphoreType.DMA((2, n)) for n in (CHUNKS, CHUNKS, 1, 16, 16, 16, 1)]
    return tuple(
        pl.pallas_call(
            partial(round_kernel, bit),
            out_shape=tuple(jax.ShapeDtypeStruct(a.shape, a.dtype) for a in state[:4]),
            in_specs=[vmem] * 6,
            out_specs=(vmem,) * 4,
            scratch_shapes=[
                pltpu.VMEM((4 * CHUNKS, CHUNK), jnp.int32),
                pltpu.VMEM((SLOTS, WIDTH), f32),
                pltpu.VMEM((SLOTS, WIDTH), f32),
                pltpu.VMEM((SLOTS, WIDTH), f32),
                pltpu.VMEM((ROWS, 2 * WIDTH), bf16),
                pltpu.VMEM((3 * SLOTS, WIDTH), f32),
                pltpu.VMEM((3 * SLOTS, 2 * WIDTH), bf16),
                pltpu.VMEM((RELS, SLOTS), bf16),
                pltpu.VMEM((SLOTS, WIDTH), f32),
                pltpu.VMEM((RELS, 2 * WIDTH), bf16),
                pltpu.VMEM((CHUNKS, SLOTS, CHUNK), f32),
                pltpu.VMEM((SLOTS, 2 * WIDTH), bf16),
                pltpu.VMEM((SLOTS, 2 * WIDTH), bf16),
                pltpu.VMEM((SLOTS, 2 * WIDTH), bf16),
                pltpu.VMEM((SLOTS, 2 * WIDTH), bf16),
                pltpu.VMEM((SLOTS, 2 * WIDTH), bf16),
                pltpu.VMEM((ROWS, WIDTH), f32),
                pltpu.VMEM((RELS, WIDTH), f32),
                pltpu.VMEM((HALF, WIDTH), f32),
                pltpu.VMEM((HALF, WIDTH), f32),
                pltpu.VMEM((16, PIECE, WIDTH), f32),
                pltpu.VMEM((16, PIECE, WIDTH), f32),
                pltpu.VMEM((RELS, WIDTH), f32),
                *sems,
            ],
            compiler_params=pltpu.CompilerParams(
                collective_id=bit, has_side_effects=True, vmem_limit_bytes=48 * 1024 * 1024
            ),
        )(*state)
    )


def ids_kernel(counts_ref, src_ref, tgt_ref, rel_ref, neg_ref, *rest):
    own, others, sems = rest[:ROUNDS], rest[ROUNDS : 2 * ROUNDS], rest[2 * ROUNDS]
    me = lax.axis_index("dom")
    partners = []
    for bit in range(BITS):
        distance = 1 << bit
        partners.append((me + distance - 2 * distance * ((me // distance) % 2),))
    barrier = pltpu.get_barrier_semaphore()
    for partner in partners:
        pl.semaphore_signal(barrier, inc=1, device_id=partner, device_id_type=pl.DeviceIdType.MESH)
    for r in range(ROUNDS):
        for c in range(CHUNKS):
            lanes = slice(c * CHUNK, (c + 1) * CHUNK)
            slots = lax.broadcasted_iota(jnp.int32, (1, CHUNK), 1) + c * CHUNK
            kinds = jnp.where(slots < counts_ref[:, r : r + 1], rel_ref[r : r + 1, lanes], -1)
            own[r][SRC * CHUNKS + c : SRC * CHUNKS + c + 1, :] = src_ref[r : r + 1, lanes]
            own[r][TGT * CHUNKS + c : TGT * CHUNKS + c + 1, :] = tgt_ref[r : r + 1, lanes]
            own[r][NEG * CHUNKS + c : NEG * CHUNKS + c + 1, :] = neg_ref[r, :, lanes]
            own[r][REL * CHUNKS + c : REL * CHUNKS + c + 1, :] = kinds
    pl.semaphore_wait(barrier, BITS)
    copies = []
    for r in range(ROUNDS):
        for bit in range(BITS):
            copies.append(
                pltpu.make_async_remote_copy(
                    src_ref=own[r],
                    dst_ref=others[r].at[bit],
                    send_sem=sems.at[0, r * BITS + bit],
                    recv_sem=sems.at[1, r * BITS + bit],
                    device_id=partners[bit],
                    device_id_type=pl.DeviceIdType.MESH,
                )
            )
    for copy in copies:
        copy.start()
    for copy in copies:
        copy.wait()


def trade_ids(*arrays):
    vmem = pl.BlockSpec(memory_space=pltpu.VMEM)
    own = [jax.ShapeDtypeStruct((4 * CHUNKS, CHUNK), jnp.int32)] * ROUNDS
    others = [jax.ShapeDtypeStruct((BITS, 4 * CHUNKS, CHUNK), jnp.int32)] * ROUNDS
    made = pl.pallas_call(
        ids_kernel,
        out_shape=(*own, *others),
        in_specs=[vmem] * len(arrays),
        out_specs=(vmem,) * (2 * ROUNDS),
        scratch_shapes=[pltpu.SemaphoreType.DMA((2, ROUNDS * BITS))],
        compiler_params=pltpu.CompilerParams(collective_id=BITS, has_side_effects=True),
    )(*arrays)
    return made[:ROUNDS], made[ROUNDS:]


def local(
    embeddings,
    row_state,
    relations,
    rel_state,
    plan,
    edge_counts,
    sources,
    targets,
    relation_ids,
    negatives,
):
    own, others = trade_ids(edge_counts.T, sources, targets, relation_ids, negatives)
    state = (embeddings, row_state.reshape(-1, CHUNK), relations, rel_state.reshape(-1, CHUNK))
    branches = [partial(run_round, bit=bit) for bit in range(BITS)]
    for r in range(ROUNDS):
        state = lax.switch(plan[r], branches, (*state, own[r], others[r]))
    embeddings, row_state, relations, rel_state = state
    return (embeddings, row_state.reshape(-1), relations, rel_state.reshape(-1))


def solution(mesh):
    placed = (
        P("dom", None),
        P("dom"),
        P(),
        P(),
        P(),
        P(None, "dom"),
        P(None, "dom"),
        P(None, "dom"),
        P(None, "dom"),
        P(None, "dom", None),
    )
    return jax.shard_map(
        local,
        mesh=mesh,
        in_specs=placed,
        out_specs=(P("dom", None), P("dom"), P(), P()),
        check_vma=False,
    )
```
